512 devices in a mesh: tm: 64 (over z, x_hi, core), mic: 8 (over x_lo, y).
Axes of the slice: x: 4 (x_hi: 2, x_lo: 2; x = x_hi * 2 + x_lo), y: 4, z: 16, core: 2. Of those that a mesh axis runs over, the one named last changes fastest.
Arguments:
- signal: bfloat16 [262144, 4096], P('tm', 'mic')
- mic_pos: int32 [3, 4096], P(None, 'mic'), may hold values from 0 to 255, as said below
- grid_pos: int32 [3, 8192], replicated, may hold values from 0 to 255, as said below
- bins: int32 [2], replicated, may hold values from 1 to 511, as said below
Outputs:
- power: float32 [8192], P('mic')
The draws below stay inside these ranges and needn't reach their ends.
Inputs may be any that keep to these rules, and one draw needn't show every extreme that they name: `mic_pos`: rows are x, y, z; a microphone's z is below 16. `grid_pos`: rows are x, y, z; a grid point's z is 64 or more and below 128. `bins`: the bin indices are distinct; the first is 511.
All inputs are finite; a program needn't handle non-finite values.
Results may differ from the reference program's by a relative error of at most 0.0006.
The reference program's roundings to bfloat16 on the way (of `fourier` and `spectra`) count: a program that leaves them out, or rounds other values in their place, can miss the bound.
Values may be sent and summed in bfloat16 or wider, within the bound.
A program may use at most 64 MiB of HBM per device.

```python
import math
import jax
import jax.numpy as jnp
from jax import lax

MICS = 4096
SEGLEN = 8192
NBINS = 2
GRID = 8192
SPAN = 4096
TIME = 262144


def draw_signal(key, part):
    first_key, second_key, third_key = jax.random.split(key, 3)
    mic_gains = 10.0 ** jax.random.uniform(second_key, (1, MICS), jnp.float32, 0.0, 1.0)
    envelope = 1.0 + 2.0 * jnp.arange(TIME, dtype=jnp.float32)[:, None] / TIME
    common = jax.random.normal(third_key, (TIME, 1), jnp.float32)
    samples = jax.random.normal(first_key, (TIME, MICS), jnp.float32)
    samples = samples + common
    return (samples * mic_gains * envelope).astype(jnp.bfloat16)


def draw_mic_pos(key, part):
    plane_key, depth_key = jax.random.split(jax.random.fold_in(key, 11))
    plane = jax.random.randint(plane_key, (2, MICS), 0, 256, jnp.int32)
    depth = jax.random.randint(depth_key, (1, MICS), 0, 16, jnp.int32)
    return jnp.concatenate([plane, depth], axis=0)


def draw_grid_pos(key, part):
    plane_key, depth_key = jax.random.split(jax.random.fold_in(key, 23))
    plane = jax.random.randint(plane_key, (2, GRID), 0, 256, jnp.int32)
    depth = jax.random.randint(depth_key, (1, GRID), 64, 128, jnp.int32)
    return jnp.concatenate([plane, depth], axis=0)


def draw_bins(key, part):
    key = jax.random.fold_in(key, 37)
    largest = SEGLEN // 16 - 1
    order = jax.random.permutation(key, jnp.arange(largest - 1, dtype=jnp.int32))
    rest = order[:NBINS - 1] + 1
    return jnp.concatenate([jnp.full((1,), largest, jnp.int32), rest], axis=0)


def setup_inputs(seed: int = 0) -> dict:
    splits = jax.random.split(jax.random.key(seed), 5)
    signal = draw_signal(jax.random.fold_in(splits[4], 71), 0)
    mic_pos = draw_mic_pos(jax.random.fold_in(splits[4], 71), 0)
    grid_pos = draw_grid_pos(jax.random.fold_in(splits[4], 71), 0)
    bins = draw_bins(jax.random.fold_in(splits[4], 71), 0)
    return {"signal": signal, "mic_pos": mic_pos, "grid_pos": grid_pos, "bins": bins}


def fourier_rows(bins):
    sample_index = jnp.arange(SEGLEN, dtype=jnp.int32)
    window = 0.5 - 0.5 * jnp.cos(2.0 * math.pi * sample_index.astype(jnp.float32) / SEGLEN)
    phases = bins[:, None] * sample_index[None, :] % SEGLEN
    angles = 2.0 * math.pi * phases.astype(jnp.float32) / SEGLEN
    weighting = window / math.sqrt(0.375 * SEGLEN)
    fourier = jnp.stack([weighting * jnp.cos(angles), -weighting * jnp.sin(angles)], axis=1)
    return fourier.reshape(2 * NBINS, SEGLEN).astype(jnp.bfloat16)

def steer_block(points, mic_pos, bins):
    offsets = points[:, :, None] - mic_pos[:, None, :]
    distance = jnp.sqrt(lax.optimization_barrier(jnp.sum(offsets * offsets, axis=0)).astype(jnp.float32))
    strength = 16.0 / distance
    cycles = bins.astype(jnp.float32)[:, None, None] * distance[None] * (16.0 / SEGLEN)
    cosine_part = (strength[None] * jnp.cos(2.0 * math.pi * cycles)).astype(jnp.bfloat16)
    sine_part = (strength[None] * jnp.sin(2.0 * math.pi * cycles)).astype(jnp.bfloat16)
    return (cosine_part, sine_part)

def steered(spectra, cosine_part, sine_part):
    segments = spectra.shape[0]
    mic_count = spectra.shape[2]
    width = cosine_part.shape[1]
    per_bin = []
    for bin_index in range(NBINS):
        bin_pair = spectra[:, 2 * bin_index:2 * bin_index + 2, :].reshape(2 * segments, mic_count)
        cosine_sum = jnp.dot(bin_pair, cosine_part[bin_index].T, preferred_element_type=jnp.float32).reshape(segments, 2, width)
        sine_sum = jnp.dot(bin_pair, sine_part[bin_index].T, preferred_element_type=jnp.float32).reshape(segments, 2, width)
        real_part = cosine_sum[:, 0] - sine_sum[:, 1]
        imag_part = cosine_sum[:, 1] + sine_sum[:, 0]
        per_bin.append(jnp.stack([real_part, imag_part], axis=1))
    return jnp.stack(per_bin, axis=1)

def reference(signal, mic_pos, grid_pos, bins):
    fourier = fourier_rows(bins)
    segment_count = TIME // SPAN
    blocks = signal.reshape(segment_count, SPAN, MICS)

    def segment_spectrum(index):
        first_half = lax.dynamic_index_in_dim(blocks, index, 0, keepdims=False)
        later = jnp.minimum(index + 1, segment_count - 1).astype(jnp.int32)
        second_half = lax.dynamic_index_in_dim(blocks, later, 0, keepdims=False)
        second_half = jnp.where(index + 1 < segment_count, second_half, jnp.zeros_like(second_half))
        segment = jnp.concatenate([first_half, second_half], axis=0)
        return jnp.dot(fourier, segment, preferred_element_type=jnp.float32)
    spectra = lax.map(segment_spectrum, jnp.arange(segment_count, dtype=jnp.int32)).astype(jnp.bfloat16)
    block_width = min(GRID, 1024)
    block_count = GRID // block_width
    points = grid_pos.reshape(3, block_count, block_width).transpose(1, 0, 2)

    def block_power(block_points):
        cosine_part, sine_part = steer_block(block_points, mic_pos, bins)
        beam = steered(spectra, cosine_part, sine_part)
        return lax.optimization_barrier(jnp.sum(beam * beam, axis=(0, 1, 2)))
    power = lax.map(block_power, points).reshape(GRID)
    return power / (segment_count * NBINS * MICS)
```

```python
import math

import jax
import jax.numpy as jnp
from jax import lax
from jax.experimental import pallas as pl
from jax.experimental.pallas import tpu as pltpu
from jax.sharding import PartitionSpec as P

MESH = pl.DeviceIdType.MESH
F32 = jnp.float32
BF16 = jnp.bfloat16

MICS = 4096
SEGLEN = 8192
NBINS = 2
SPAN = 4096
LOCAL_MICS = 512
DEPTHS = 16
PLANE = 4
OWNERS = 8
SHARE = 64
POINTS = OWNERS * SHARE
CHUNKS = 8
CHUNK = SPAN // CHUNKS
TILE = 16
EARLY = 16

SINE = (0.7071043846242844, -0.029459528423390287, 0.00036709000983827487, -2.0288338894692693e-06)
SINE_FINE = (
    0.707106764602781,
    -0.029462748844770903,
    0.0003682655953189757,
    -2.1877062853298923e-06,
    7.155046293945055e-09,
)
COSINE = (
    1.414213496370263,
    -0.17677635985529122,
    0.0036825749254888974,
    -3.061255945642025e-05,
    1.2790331792070752e-07,
)
TURN = 2.0 * math.pi
TURN_HIGH = 6.28125
TURN_LOW = TURN - TURN_HIGH
ROUNDER = 1.5 * 2.0**23


def poly(coefficients, x):
    value = coefficients[-1] * x + coefficients[-2]
    for c in coefficients[-3::-1]:
        value = value * x + c
    return value


def half_sine(f):
    return f * poly(SINE_FINE, f * f)


def table_chunk(index, bin_a, bin_b):
    row = lax.broadcasted_iota(jnp.int32, (8, CHUNK), 0)
    lane = lax.broadcasted_iota(jnp.int32, (8, CHUNK), 1)
    k = jnp.where((row & 2) == 0, bin_a, bin_b)
    sample = lane + index * CHUNK + (row >> 2) * SPAN
    phase = (k * sample + (row & 1) * (SEGLEN // 4)) & (SEGLEN - 1)
    s = half_sine((phase - SEGLEN // 2).astype(F32) * (TURN / SEGLEN))
    near = jnp.minimum(sample, SEGLEN - sample).astype(F32)
    w = half_sine(near * (TURN / SEGLEN))
    weighting = (0.5 / math.sqrt(0.375 * SEGLEN)) * (w * w)
    return (weighting * (s * s - 1.0)).astype(BF16)


def kernel(
    sig_hbm,
    mic_hbm,
    grid_hbm,
    bins_hbm,
    out_ref,
    sig,
    mic,
    grid,
    bins,
    mic_columns,
    grid_rows,
    own_half,
    next_half,
    halo,
    gathered,
    wide,
    x_ref,
    w_ref,
    part,
    arrived,
    plane,
    final,
    sig_sem,
    small_sem,
    halo_sem,
    gather_send,
    gather_recv,
    sum_send,
    sum_recv,
    plane_send,
    plane_recv,
    final_send,
    final_recv,
):
    t, j = lax.axis_index("tm"), lax.axis_index("mic")
    z, p = t // PLANE, t % PLANE
    spans = DEPTHS * PLANE
    before, after = lax.rem(t + spans - 1, spans), lax.rem(t + 1, spans)

    def depth(d):
        return lax.rem(z + d, DEPTHS) * PLANE + p

    def in_plane(d):
        return z * PLANE + lax.rem(p + d, PLANE)

    def owner(d):
        return lax.rem(j + d, OWNERS)

    small = [
        pltpu.make_async_copy(bins_hbm, bins, small_sem.at[0]),
        pltpu.make_async_copy(mic_hbm, mic, small_sem.at[1]),
        pltpu.make_async_copy(grid_hbm, grid, small_sem.at[2]),
    ]
    for copy in small:
        copy.start()
    loads = []
    for c in range(CHUNKS):
        rows = pl.ds(c * CHUNK, CHUNK)
        loads.append(pltpu.make_async_copy(sig_hbm.at[rows], sig.at[rows], sig_sem.at[c]))
        loads[-1].start()

    barrier = pltpu.get_barrier_semaphore()
    peers = [(before, j), (after, j)]
    peers += [(depth(d), j) for d in range(1, DEPTHS)]
    peers += [(in_plane(d), j) for d in range(1, PLANE)]
    peers += [(t, owner(d)) for d in range(1, OWNERS)]
    for peer in peers:
        pl.semaphore_signal(barrier, inc=1, device_id=peer, device_id_type=MESH)

    small[0].wait()
    bin_a, bin_b = bins[0], bins[1]
    tables = [table_chunk(c, bin_a, bin_b) for c in range(CHUNKS)]

    small[1].wait()
    small[2].wait()
    padded = jnp.concatenate([mic[...].astype(F32), jnp.zeros((5, LOCAL_MICS), F32)], axis=0)
    mic_columns[...] = padded.T
    odd = lax.rem(z, 2) == 1
    low_lanes = lax.broadcasted_iota(jnp.int32, (8, 128), 1) < SHARE
    window = (z // 2) * 128
    for coordinate in range(3):
        for a in range(OWNERS // 2):
            halves = []
            for side in range(2):
                start = pl.multiple_of((2 * a + side) * OWNERS * 128 + window, 128)
                row = grid[coordinate : coordinate + 1, pl.ds(start, 128)].astype(F32)
                row = jnp.broadcast_to(row, (8, 128))
                other = pltpu.roll(row, SHARE, 1)
                halves.append(jnp.where(odd, other, row) if side == 0 else jnp.where(odd, row, other))
            grid_rows[coordinate, :, a * 128 : (a + 1) * 128] = jnp.where(low_lanes, halves[0], halves[1])

    total = jnp.zeros((8, LOCAL_MICS), F32)
    for c in range(CHUNKS):
        loads[c].wait()
        total += jnp.dot(tables[c], sig[c * CHUNK : (c + 1) * CHUNK, :], preferred_element_type=F32)
    for c in range(4):
        block = total[:, c * 128 : (c + 1) * 128]
        own_half[4 * c : 4 * c + 4, :] = block[0:4]
        next_half[4 * c : 4 * c + 4, :] = block[4:8]

    pl.semaphore_wait(barrier, len(peers))
    halo_copy = pltpu.make_async_remote_copy(
        src_ref=next_half,
        dst_ref=halo,
        send_sem=halo_sem.at[0],
        recv_sem=halo_sem.at[1],
        device_id=(before, j),
        device_id_type=MESH,
    )
    halo_copy.start()

    bin_values = (bin_a.astype(F32), bin_b.astype(F32))

    def steer(step, carry):
        rows = pl.ds(pl.multiple_of(step * TILE, TILE), TILE)
        square = None
        for coordinate in range(3):
            column = mic_columns[rows, coordinate : coordinate + 1]
            points = grid_rows[coordinate, 0:1, :]
            offset = points - column
            square = offset * offset if square is None else square + offset * offset
        inverse = lax.rsqrt(square)
        distance = square * inverse
        strength = 16.0 * inverse
        for b in range(NBINS):
            angle = (bin_values[b] * distance) * (TURN / 512.0)
            turns = (angle * (1.0 / TURN) + ROUNDER) - ROUNDER
            f = (angle - turns * TURN_HIGH) - turns * TURN_LOW
            f2 = f * f
            s = f * poly(SINE, f2)
            c = poly(COSINE, f2)
            scaled = strength * s
            sine_rows = pl.ds(pl.multiple_of(step * TILE + LOCAL_MICS, TILE), TILE)
            w_ref[b, rows, :] = (strength - scaled * s).astype(BF16)
            w_ref[b, sine_rows, :] = (scaled * c).astype(BF16)
        return carry

    lax.fori_loop(0, EARLY, steer, 0)

    halo_copy.wait_recv()
    following = jnp.where(t == spans - 1, 0.0, halo[...])
    gathered[z] = (own_half[...] + following).astype(BF16)
    gather_copies = []
    for d in sorted(range(1, DEPTHS), key=lambda d: -min(d, DEPTHS - d)):
        copy = pltpu.make_async_remote_copy(
            src_ref=gathered.at[z],
            dst_ref=gathered.at[z],
            send_sem=gather_send.at[d],
            recv_sem=gather_recv.at[d],
            device_id=(depth(d), j),
            device_id_type=MESH,
        )
        copy.start()
        gather_copies.append((d, copy))

    lax.fori_loop(EARLY, LOCAL_MICS // TILE, steer, 0)

    for d in range(1, DEPTHS):
        slot = gathered.at[lax.rem(z + DEPTHS - d, DEPTHS)]
        pltpu.make_async_remote_copy(
            src_ref=slot,
            dst_ref=slot,
            send_sem=gather_send.at[d],
            recv_sem=gather_recv.at[d],
            device_id=(depth(d), j),
            device_id_type=MESH,
        ).wait_recv()

    for s in range(DEPTHS):
        wide[16 * s : 16 * s + 16, :] = gathered[s].astype(F32)
    for c in range(4):
        for b in range(NBINS):
            real = wide[pl.ds(4 * c + 2 * b, DEPTHS, stride=16), :]
            imag = wide[pl.ds(4 * c + 2 * b + 1, DEPTHS, stride=16), :]
            lanes = slice(128 * c, 128 * c + 128)
            sine_lanes = slice(LOCAL_MICS + 128 * c, LOCAL_MICS + 128 * c + 128)
            x_ref[b, 0:16, lanes] = real.astype(BF16)
            x_ref[b, 16:32, lanes] = imag.astype(BF16)
            x_ref[b, 0:16, sine_lanes] = (-imag).astype(BF16)
            x_ref[b, 16:32, sine_lanes] = real.astype(BF16)

    beams = [jnp.dot(x_ref[b], w_ref[b], preferred_element_type=F32) for b in range(NBINS)]
    low = lax.broadcasted_iota(jnp.int32, (32, 128), 1) < SHARE
    for a in range(OWNERS // 2):
        first, second = (beam[:, a * 128 : (a + 1) * 128] for beam in beams)
        part[2 * a] = jnp.where(low, first, pltpu.roll(second, SHARE, 1))
        part[2 * a + 1] = jnp.where(low, pltpu.roll(first, SHARE, 1), second)

    sum_copies = []
    for d in (4, 5, 3, 6, 2, 7, 1):
        copy = pltpu.make_async_remote_copy(
            src_ref=part.at[owner(d)],
            dst_ref=arrived.at[j],
            send_sem=sum_send.at[d],
            recv_sem=sum_recv.at[d],
            device_id=(t, owner(d)),
            device_id_type=MESH,
        )
        copy.start()
        sum_copies.append(copy)
    beam = part[j]
    for d in range(1, OWNERS):
        source = lax.rem(j + OWNERS - d, OWNERS)
        pltpu.make_async_remote_copy(
            src_ref=part.at[source],
            dst_ref=arrived.at[source],
            send_sem=sum_send.at[d],
            recv_sem=sum_recv.at[d],
            device_id=(t, owner(d)),
            device_id_type=MESH,
        ).wait_recv()
        beam += arrived[source]
    squares = beam * beam
    folded = squares[0:8] + squares[8:16] + squares[16:24] + squares[24:32]
    folded += pltpu.roll(folded, SHARE, 1)
    plane[p] = jnp.sum(folded, axis=0, keepdims=True)

    plane_copies = []
    for d in range(1, PLANE):
        copy = pltpu.make_async_remote_copy(
            src_ref=plane.at[p],
            dst_ref=plane.at[p],
            send_sem=plane_send.at[d],
            recv_sem=plane_recv.at[d],
            device_id=(in_plane(d), j),
            device_id_type=MESH,
        )
        copy.start()
        plane_copies.append(copy)
    for d in range(1, PLANE):
        slot = plane.at[lax.rem(p + PLANE - d, PLANE)]
        pltpu.make_async_remote_copy(
            src_ref=slot,
            dst_ref=slot,
            send_sem=plane_send.at[d],
            recv_sem=plane_recv.at[d],
            device_id=(in_plane(d), j),
            device_id_type=MESH,
        ).wait_recv()
    final[z] = (plane[0] + plane[1]) + (plane[2] + plane[3])

    final_copies = []
    for d in sorted(range(1, DEPTHS), key=lambda d: -min(d, DEPTHS - d)):
        copy = pltpu.make_async_remote_copy(
            src_ref=final.at[z],
            dst_ref=final.at[z],
            send_sem=final_send.at[d],
            recv_sem=final_recv.at[d],
            device_id=(depth(d), j),
            device_id_type=MESH,
        )
        copy.start()
        final_copies.append(copy)
    halo_copy.wait_send()
    for _, copy in gather_copies:
        copy.wait_send()
    for copy in sum_copies + plane_copies + final_copies:
        copy.wait_send()
    for d in range(1, DEPTHS):
        slot = final.at[lax.rem(z + DEPTHS - d, DEPTHS)]
        pltpu.make_async_remote_copy(
            src_ref=slot,
            dst_ref=slot,
            send_sem=final_send.at[d],
            recv_sem=final_recv.at[d],
            device_id=(depth(d), j),
            device_id_type=MESH,
        ).wait_recv()
    first_lanes = lax.broadcasted_iota(jnp.int32, (1, 128), 1) < SHARE
    scale = 1.0 / (spans * NBINS * MICS)
    for r in range(DEPTHS // 2):
        out_ref[r : r + 1, :] = jnp.where(first_lanes, final[2 * r], final[2 * r + 1]) * scale


def local(signal, mic_pos, grid_pos, bins):
    hbm = pl.BlockSpec(memory_space=pl.ANY)
    dma = pltpu.SemaphoreType.DMA
    power = pl.pallas_call(
        kernel,
        out_shape=jax.ShapeDtypeStruct((DEPTHS // 2, 128), F32),
        in_specs=[hbm] * 4,
        out_specs=pl.BlockSpec(memory_space=pltpu.VMEM),
        scratch_shapes=[
            pltpu.VMEM((SPAN, LOCAL_MICS), BF16),
            pltpu.VMEM(mic_pos.shape, jnp.int32),
            pltpu.VMEM(grid_pos.shape, jnp.int32),
            pltpu.SMEM(bins.shape, jnp.int32),
            pltpu.VMEM((LOCAL_MICS, 8), F32),
            pltpu.VMEM((3, 8, POINTS), F32),
            pltpu.VMEM((16, 128), F32),
            pltpu.VMEM((16, 128), F32),
            pltpu.VMEM((16, 128), F32),
            pltpu.VMEM((DEPTHS, 16, 128), BF16),
            pltpu.VMEM((DEPTHS * 16, 128), F32),
            pltpu.VMEM((NBINS, 2 * DEPTHS, 2 * LOCAL_MICS), BF16),
            pltpu.VMEM((NBINS, 2 * LOCAL_MICS, POINTS), BF16),
            pltpu.VMEM((OWNERS, 2 * DEPTHS, 128), F32),
            pltpu.VMEM((OWNERS, 2 * DEPTHS, 128), F32),
            pltpu.VMEM((PLANE, 1, 128), F32),
            pltpu.VMEM((DEPTHS, 1, 128), F32),
            dma((CHUNKS,)),
            dma((3,)),
            dma((2,)),
            dma((DEPTHS,)),
            dma((DEPTHS,)),
            dma((OWNERS,)),
            dma((OWNERS,)),
            dma((PLANE,)),
            dma((PLANE,)),
            dma((DEPTHS,)),
            dma((DEPTHS,)),
        ],
        compiler_params=pltpu.CompilerParams(
            collective_id=0, has_side_effects=True, vmem_limit_bytes=32 * 1024 * 1024
        ),
    )(signal, mic_pos, grid_pos, bins)
    return power.reshape(-1)


def solution(mesh):
    in_specs = (P("tm", "mic"), P(None, "mic"), P(), P())
    out_specs = P("mic")
    return jax.shard_map(local, mesh=mesh, in_specs=in_specs, out_specs=out_specs, check_vma=False)
```

```python
import math

import jax
import jax.numpy as jnp
from jax import lax
from jax.experimental import pallas as pl
from jax.experimental.pallas import tpu as pltpu
from jax.sharding import PartitionSpec as P

MESH = pl.DeviceIdType.MESH
F32 = jnp.float32
BF16 = jnp.bfloat16

MICS = 4096
SEGLEN = 8192
NBINS = 2
SPAN = 4096
LOCAL_MICS = 512
SPANS = 64
GROUP = 8
GROUPS = SPANS // GROUP
OWNERS = 8
SHARE = 128
POINTS = OWNERS * SHARE
CHUNKS = 8
CHUNK = SPAN // CHUNKS
TILE = 32
WIDTH = 512
TILES = LOCAL_MICS // TILE
STEPS = TILES * POINTS // WIDTH
EARLY = 4

SINE = (0.7071043846242844, -0.029459528423390287, 0.00036709000983827487, -2.0288338894692693e-06)
SINE_FINE = (
    0.707106764602781,
    -0.029462748844770903,
    0.0003682655953189757,
    -2.1877062853298923e-06,
    7.155046293945055e-09,
)
COSINE = (
    1.414213496370263,
    -0.17677635985529122,
    0.0036825749254888974,
    -3.061255945642025e-05,
    1.2790331792070752e-07,
)
TURN = 2.0 * math.pi
TURN_HIGH = 6.28125
TURN_LOW = TURN - TURN_HIGH
ROUNDER = 1.5 * 2.0**23


def poly(coefficients, x):
    value = coefficients[-1] * x + coefficients[-2]
    for c in coefficients[-3::-1]:
        value = value * x + c
    return value


def half_sine(f):
    return f * poly(SINE_FINE, f * f)


def table_chunk(index, bin_a, bin_b):
    row = lax.broadcasted_iota(jnp.int32, (8, CHUNK), 0)
    lane = lax.broadcasted_iota(jnp.int32, (8, CHUNK), 1)
    k = jnp.where((row & 2) == 0, bin_a, bin_b)
    sample = lane + index * CHUNK + (row >> 2) * SPAN
    phase = (k * sample + (row & 1) * (SEGLEN // 4)) & (SEGLEN - 1)
    s = half_sine((phase - SEGLEN // 2).astype(F32) * (TURN / SEGLEN))
    near = jnp.minimum(sample, SEGLEN - sample).astype(F32)
    w = half_sine(near * (TURN / SEGLEN))
    weighting = (0.5 / math.sqrt(0.375 * SEGLEN)) * (w * w)
    return (weighting * (s * s - 1.0)).astype(BF16)


def flip(index, bits, mask):
    value = 0
    for bit in range(bits):
        digit = (index // (1 << bit)) % 2
        value = value + (1 << bit) * (1 - digit if mask >> bit & 1 else digit)
    return value


def kernel(
    sig_hbm,
    mic_hbm,
    grid_hbm,
    bins_hbm,
    out_ref,
    sig,
    mic,
    grid,
    bins,
    mic_columns,
    grid_rows,
    halves,
    following,
    wide,
    x_ref,
    w_ref,
    part,
    arrived,
    final,
    sig_sem,
    small_sem,
    lead_send,
    lead_recv,
    group_send,
    group_recv,
    sum_send,
    sum_recv,
    final_send,
    final_recv,
    far_sem,
):
    t, j = lax.axis_index("tm"), lax.axis_index("mic")
    k, g = t // GROUP, t % GROUP

    def member(mask):
        return k * GROUP + flip(g, 3, mask)

    def column(d):
        return lax.rem(t + SPANS + d * GROUP, SPANS)

    small = [
        pltpu.make_async_copy(bins_hbm, bins, small_sem.at[0]),
        pltpu.make_async_copy(mic_hbm, mic, small_sem.at[1]),
        pltpu.make_async_copy(grid_hbm, grid, small_sem.at[2]),
    ]
    for copy in small:
        copy.start()
    loads = []
    for c in range(CHUNKS):
        rows = pl.ds(c * CHUNK, CHUNK)
        loads.append(pltpu.make_async_copy(sig_hbm.at[rows], sig.at[rows], sig_sem.at[c]))
        loads[-1].start()

    barrier = pltpu.get_barrier_semaphore()
    next_leader = lax.rem(k + 1, GROUPS) * GROUP
    near = [(column(d), j) for d in (-2, 2, -1, 1)]
    near += [(member(m), j) for m in (7, 6, 3, 2, 5, 4, 1)]
    near += [(t, lax.rem(j + d, OWNERS)) for d in range(1, OWNERS)]
    for peer in [(next_leader, j)] + near:
        pl.semaphore_signal(barrier, inc=1, device_id=peer, device_id_type=MESH)

    small[0].wait()
    bin_a, bin_b = bins[0], bins[1]
    tables = [table_chunk(c, bin_a, bin_b) for c in range(CHUNKS)]

    small[1].wait()
    small[2].wait()
    padded = jnp.concatenate([mic[...].astype(F32), jnp.zeros((5, LOCAL_MICS), F32)], axis=0)
    mic_columns[...] = padded.T
    for o in range(OWNERS):
        start = pl.multiple_of((o * GROUP + g) * SHARE, SHARE)
        for coordinate in range(3):
            row = grid[coordinate : coordinate + 1, pl.ds(start, SHARE)].astype(F32)
            grid_rows[coordinate : coordinate + 1, o * SHARE : (o + 1) * SHARE] = row

    bin_values = (bin_a.astype(F32), bin_b.astype(F32))

    def steer(step, carry):
        tile, side = step % TILES, step // TILES
        rows = pl.ds(pl.multiple_of(tile * TILE, TILE), TILE)
        sine_rows = pl.ds(pl.multiple_of(tile * TILE + LOCAL_MICS, TILE), TILE)
        lanes = pl.ds(pl.multiple_of(side * WIDTH, WIDTH), WIDTH)
        square = None
        for coordinate in range(3):
            column = mic_columns[rows, coordinate : coordinate + 1]
            offset = grid_rows[coordinate : coordinate + 1, lanes] - column
            square = offset * offset if square is None else square + offset * offset
        inverse = lax.rsqrt(square)
        distance = square * inverse
        strength = 16.0 * inverse
        for b in range(NBINS):
            angle = (bin_values[b] * distance) * (TURN / 512.0)
            turns = (angle * (1.0 / TURN) + ROUNDER) - ROUNDER
            f = (angle - turns * TURN_HIGH) - turns * TURN_LOW
            f2 = f * f
            s = f * poly(SINE, f2)
            c = poly(COSINE, f2)
            scaled = strength * s
            w_ref[b, rows, lanes] = (strength - scaled * s).astype(BF16)
            w_ref[b, sine_rows, lanes] = (scaled * c).astype(BF16)
        return carry

    lax.fori_loop(0, EARLY, steer, 0)

    total = jnp.zeros((8, LOCAL_MICS), F32)
    for c in range(CHUNKS):
        loads[c].wait()
        total += jnp.dot(tables[c], sig[c * CHUNK : (c + 1) * CHUNK, :], preferred_element_type=F32)
    for c in range(4):
        block = total[:, c * 128 : (c + 1) * 128]
        halves[g, 0, 4 * c : 4 * c + 4, :] = block[0:4]
        halves[g, 1, 4 * c : 4 * c + 4, :] = block[4:8]

    leader = g == 0
    pl.semaphore_wait(barrier, jnp.where(leader, len(near) + GROUP, len(near)))
    previous = lax.rem(k + GROUPS - 1, GROUPS) * GROUP
    lead_copies = [
        pltpu.make_async_remote_copy(
            src_ref=halves.at[0, 1],
            dst_ref=following,
            send_sem=lead_send.at[i],
            recv_sem=lead_recv,
            device_id=(previous + i, j),
            device_id_type=MESH,
        )
        for i in range(GROUP)
    ]

    @pl.when(leader)
    def _():
        for copy in lead_copies:
            copy.start()

    group_copies = []
    for m in (7, 6, 3, 2, 5, 4, 1):
        copy = pltpu.make_async_remote_copy(
            src_ref=halves.at[g],
            dst_ref=halves.at[g],
            send_sem=group_send.at[m],
            recv_sem=group_recv.at[m],
            device_id=(member(m), j),
            device_id_type=MESH,
        )
        copy.start()
        group_copies.append(copy)
    for d in (-2, 2):
        pl.semaphore_signal(far_sem.at[0], inc=1, device_id=(column(d), j), device_id_type=MESH)

    lax.fori_loop(EARLY, STEPS, steer, 0)

    pl.semaphore_wait(far_sem.at[0], 2)
    for m in range(1, GROUP):
        pl.semaphore_signal(far_sem.at[1], inc=1, device_id=(member(m), j), device_id_type=MESH)

    for m in (1, 4, 5, 2, 3, 6, 7):
        slot = halves.at[flip(g, 3, m)]
        pltpu.make_async_remote_copy(
            src_ref=slot,
            dst_ref=slot,
            send_sem=group_send.at[m],
            recv_sem=group_recv.at[m],
            device_id=(member(m), j),
            device_id_type=MESH,
        ).wait_recv()
    lead_copies[0].wait_recv()

    for s in range(GROUP):
        if s < GROUP - 1:
            second = halves[s + 1, 1]
        else:
            second = jnp.where(k == GROUPS - 1, 0.0, following[...])
        wide[16 * s : 16 * s + 16, :] = halves[s, 0] + second
    for c in range(4):
        for b in range(NBINS):
            real = wide[pl.ds(4 * c + 2 * b, GROUP, stride=16), :]
            imag = wide[pl.ds(4 * c + 2 * b + 1, GROUP, stride=16), :]
            lanes = slice(128 * c, 128 * c + 128)
            sine_lanes = slice(LOCAL_MICS + 128 * c, LOCAL_MICS + 128 * c + 128)
            x_ref[b, :, lanes] = jnp.concatenate([real, imag], axis=0).astype(BF16)
            x_ref[b, :, sine_lanes] = jnp.concatenate([-imag, real], axis=0).astype(BF16)

    def start_sum(destination):
        copy = pltpu.make_async_remote_copy(
            src_ref=part.at[destination],
            dst_ref=arrived.at[j],
            send_sem=sum_send.at[destination],
            recv_sem=sum_recv.at[j],
            device_id=(t, destination),
            device_id_type=MESH,
        )
        copy.start()
        return copy

    sum_copies = []
    for mask in (3, 1, 2, 0):
        pair = flip(j // 2, 2, mask)
        lanes = pl.ds(pl.multiple_of(pair * 2 * SHARE, 2 * SHARE), 2 * SHARE)
        for b in range(NBINS):
            beam = jnp.dot(x_ref[b], w_ref[b, :, lanes], preferred_element_type=F32)
            part[2 * pair, 16 * b : 16 * b + 16, :] = beam[:, :SHARE]
            part[2 * pair + 1, 16 * b : 16 * b + 16, :] = beam[:, SHARE:]
        if mask:
            sum_copies += [start_sum(2 * pair), start_sum(2 * pair + 1)]
        else:
            sum_copies.append(start_sum(2 * pair + 1 - j % 2))
    beam = part[j]
    for d in range(1, OWNERS):
        source = lax.rem(j + OWNERS - d, OWNERS)
        pltpu.make_async_remote_copy(
            src_ref=part.at[source],
            dst_ref=arrived.at[source],
            send_sem=sum_send.at[source],
            recv_sem=sum_recv.at[source],
            device_id=(t, source),
            device_id_type=MESH,
        ).wait_recv()
        beam += arrived[source]
    squares = beam * beam
    folded = squares[0:8] + squares[8:16] + squares[16:24] + squares[24:32]
    final[t] = jnp.sum(folded, axis=0, keepdims=True)

    pl.semaphore_wait(far_sem.at[1], GROUP - 1)
    for d in sorted(range(1, SPANS), key=lambda d: -min(d, SPANS - d)):
        pltpu.make_async_remote_copy(
            src_ref=final.at[t],
            dst_ref=final.at[t],
            send_sem=final_send,
            recv_sem=final_recv,
            device_id=(lax.rem(t + d, SPANS), j),
            device_id_type=MESH,
        ).start()

    @pl.when(leader)
    def _():
        for copy in lead_copies:
            copy.wait_send()

    for copy in group_copies + sum_copies:
        copy.wait_send()
    others = final.at[pl.ds(0, SPANS - 1)]
    rest = pltpu.make_async_remote_copy(
        src_ref=others,
        dst_ref=others,
        send_sem=final_send,
        recv_sem=final_recv,
        device_id=(column(1), j),
        device_id_type=MESH,
    )
    rest.wait_send()
    rest.wait_recv()
    scale = 1.0 / (SPANS * NBINS * MICS)
    for i in range(GROUP):
        row = final[i]
        for n in range(1, GROUPS):
            row += final[GROUP * n + i]
        out_ref[i : i + 1, :] = row * scale


def local(signal, mic_pos, grid_pos, bins):
    dma = pltpu.SemaphoreType.DMA
    operands = [pltpu.with_memory_space_constraint(a, pltpu.HBM) for a in (signal, mic_pos, grid_pos, bins)]
    power = pl.pallas_call(
        kernel,
        out_shape=pltpu.VMEM((GROUP, SHARE), F32),
        in_specs=[pl.BlockSpec(memory_space=pl.ANY)] * 4,
        out_specs=pl.BlockSpec(memory_space=pltpu.VMEM),
        scratch_shapes=[
            pltpu.VMEM((SPAN, LOCAL_MICS), BF16),
            pltpu.VMEM(mic_pos.shape, jnp.int32),
            pltpu.VMEM(grid_pos.shape, jnp.int32),
            pltpu.SMEM(bins.shape, jnp.int32),
            pltpu.VMEM((LOCAL_MICS, 8), F32),
            pltpu.VMEM((8, POINTS), F32),
            pltpu.VMEM((GROUP, 2, 16, 128), F32),
            pltpu.VMEM((16, 128), F32),
            pltpu.VMEM((GROUP * 16, 128), F32),
            pltpu.VMEM((NBINS, 2 * GROUP, 2 * LOCAL_MICS), BF16),
            pltpu.VMEM((NBINS, 2 * LOCAL_MICS, POINTS), BF16),
            pltpu.VMEM((OWNERS, 4 * GROUP, SHARE), F32),
            pltpu.VMEM((OWNERS, 4 * GROUP, SHARE), F32),
            pltpu.VMEM((SPANS, 1, SHARE), F32),
            dma((CHUNKS,)),
            dma((3,)),
            dma((GROUP,)),
            dma,
            dma((GROUP,)),
            dma((GROUP,)),
            dma((OWNERS,)),
            dma((OWNERS,)),
            dma,
            dma,
            pltpu.SemaphoreType.REGULAR((2,)),
        ],
        compiler_params=pltpu.CompilerParams(
            collective_id=0, has_side_effects=True, vmem_limit_bytes=32 * 1024 * 1024
        ),
    )(*operands)
    return power.reshape(-1)


def solution(mesh):
    in_specs = (P("tm", "mic"), P(None, "mic"), P(), P())
    out_specs = P("mic")
    return jax.shard_map(local, mesh=mesh, in_specs=in_specs, out_specs=out_specs, check_vma=False)
```

```python
import math

import jax
import jax.numpy as jnp
from jax import lax
from jax.experimental import pallas as pl
from jax.experimental.pallas import tpu as pltpu
from jax.sharding import PartitionSpec as P

MESH = pl.DeviceIdType.MESH
F32 = jnp.float32
BF16 = jnp.bfloat16

MICS = 4096
SEGLEN = 8192
NBINS = 2
SPAN = 4096
LOCAL_MICS = 512
SPANS = 64
GROUP = 8
GROUPS = SPANS // GROUP
OWNERS = 8
SHARE = 128
POINTS = OWNERS * SHARE
CHUNKS = 8
CHUNK = SPAN // CHUNKS
TILE = 64
PAIR = 2 * SHARE
TILES = LOCAL_MICS // TILE
STEPS = TILES * OWNERS // 2
PORTIONS = ((0, 6), (6, 8))

UNIT = 544.5
SINE = (-0.020778089505148072, 0.22160904131003262, -0.7069151550432146, 1.0)
COSINE = (0.0025972698674584724, -0.08311238928243203, 0.4432205811375266, -0.9426014873154713, 1.0)
SINE_FINE = (
    0.707106764602781,
    -0.029462748844770903,
    0.0003682655953189757,
    -2.1877062853298923e-06,
    7.155046293945055e-09,
)
TURN = 2.0 * math.pi
TURN_HIGH = 6.28125
TURN_LOW = TURN - TURN_HIGH
ROUNDER = 1.5 * 2.0**23


def poly(coefficients, x):
    value = x if coefficients[-1] == 1.0 else coefficients[-1] * x
    value = value + coefficients[-2]
    for c in coefficients[-3::-1]:
        value = value * x + c
    return value


def half_sine(f):
    return f * poly(SINE_FINE, f * f)


def table_chunk(index, bin_a, bin_b):
    row = lax.broadcasted_iota(jnp.int32, (8, CHUNK), 0)
    lane = lax.broadcasted_iota(jnp.int32, (8, CHUNK), 1)
    k = jnp.where((row & 2) == 0, bin_a, bin_b)
    sample = lane + index * CHUNK + (row >> 2) * SPAN
    phase = (k * sample + (row & 1) * (SEGLEN // 4)) & (SEGLEN - 1)
    s = half_sine((phase - SEGLEN // 2).astype(F32) * (TURN / SEGLEN))
    near = jnp.minimum(sample, SEGLEN - sample).astype(F32)
    w = half_sine(near * (TURN / SEGLEN))
    weighting = (0.5 / math.sqrt(0.375 * SEGLEN)) * (w * w)
    return (weighting * (s * s - 1.0)).astype(BF16)


def flip(index, bits, mask):
    value = 0
    for bit in range(bits):
        digit = (index // (1 << bit)) % 2
        value = value + (1 << bit) * (1 - digit if mask >> bit & 1 else digit)
    return value


def kernel(
    sig_hbm,
    mic_hbm,
    grid_hbm,
    bins_hbm,
    out_ref,
    sig,
    mic,
    grid,
    bins,
    mic_columns,
    grid_rows,
    halves,
    following,
    wide,
    x_ref,
    w_ref,
    part,
    arrived,
    final,
    sig_sem,
    small_sem,
    lead_send,
    lead_recv,
    group_send,
    group_recv,
    sum_send,
    sum_recv,
    final_send,
    final_recv,
    far_sem,
):
    t, j = lax.axis_index("tm"), lax.axis_index("mic")
    k, g = t // GROUP, t % GROUP

    def member(mask):
        return k * GROUP + flip(g, 3, mask)

    def owner(place):
        across, along = ((1, 2), (1, 1), (1, 3), (0, 2), (1, 0), (0, 1), (0, 3), (0, 0))[place]
        return flip(j // 4, 1, across) * 4 + lax.rem(j + along, 4)

    def column(d):
        return lax.rem(t + SPANS + d * GROUP, SPANS)

    small = [
        pltpu.make_async_copy(bins_hbm, bins, small_sem.at[0]),
        pltpu.make_async_copy(mic_hbm, mic, small_sem.at[1]),
        pltpu.make_async_copy(grid_hbm, grid, small_sem.at[2]),
    ]
    for copy in small:
        copy.start()
    loads = []
    for c in range(CHUNKS):
        rows = pl.ds(c * CHUNK, CHUNK)
        loads.append(pltpu.make_async_copy(sig_hbm.at[rows], sig.at[rows], sig_sem.at[c]))
        loads[-1].start()

    barrier = pltpu.get_barrier_semaphore()
    next_leader = lax.rem(k + 1, GROUPS) * GROUP
    near = [(column(d), j) for d in (-2, 2, -1, 1)]
    near += [(member(m), j) for m in (7, 6, 3, 2, 5, 4, 1)]
    near += [(t, lax.rem(j + d, OWNERS)) for d in range(1, OWNERS)]
    for peer in [(next_leader, j)] + near:
        pl.semaphore_signal(barrier, inc=1, device_id=peer, device_id_type=MESH)

    small[0].wait()
    bin_a, bin_b = bins[0], bins[1]
    tables = [table_chunk(c, bin_a, bin_b) for c in range(CHUNKS)]

    small[1].wait()
    small[2].wait()
    padded = jnp.concatenate([mic[...].astype(F32), jnp.zeros((5, LOCAL_MICS), F32)], axis=0)
    mic_columns[...] = padded.T
    for o in range(OWNERS):
        start = pl.multiple_of((owner(o) * GROUP + g) * SHARE, SHARE)
        for coordinate in range(3):
            row = grid[coordinate : coordinate + 1, pl.ds(start, SHARE)].astype(F32)
            grid_rows[coordinate : coordinate + 1, o * SHARE : (o + 1) * SHARE] = row

    bin_values = (bin_a.astype(F32), bin_b.astype(F32))

    def steer(step, carry):
        tile, pair = step % TILES, step // TILES
        rows = pl.ds(pl.multiple_of(tile * TILE, TILE), TILE)
        sine_rows = pl.ds(pl.multiple_of(tile * TILE + LOCAL_MICS, TILE), TILE)
        lanes = pl.ds(pl.multiple_of(pair * PAIR, PAIR), PAIR)
        square = None
        for coordinate in range(3):
            column = mic_columns[rows, coordinate : coordinate + 1]
            offset = grid_rows[coordinate : coordinate + 1, lanes] - column
            square = offset * offset if square is None else square + offset * offset
        inverse = lax.rsqrt(square)
        distance = square * inverse
        strength = 16.0 * inverse
        weight = (16.0 * UNIT * UNIT) * inverse
        for b in range(NBINS):
            angle = (bin_values[b] * distance) * (-TURN / 8192.0)
            turns = (angle * (16.0 / TURN) + ROUNDER) - ROUNDER
            h = (angle - turns * (TURN_HIGH / 16.0)) - turns * (TURN_LOW / 16.0)
            h2 = h * h
            s = h * poly(SINE, h2)
            c = poly(COSINE, h2)
            scaled = weight * s
            w_ref[b, rows, lanes] = (strength - scaled * s).astype(BF16)
            w_ref[b, sine_rows, lanes] = (scaled * c).astype(BF16)
        return carry

    total = jnp.zeros((8, LOCAL_MICS), F32)
    for c in range(CHUNKS):
        loads[c].wait()
        total += jnp.dot(tables[c], sig[c * CHUNK : (c + 1) * CHUNK, :], preferred_element_type=F32)
        steer(c, 0)
    for c in range(4):
        block = total[:, c * 128 : (c + 1) * 128]
        halves[g, 0, 4 * c : 4 * c + 4, :] = block[0:4]
        halves[g, 1, 4 * c : 4 * c + 4, :] = block[4:8]

    leader = g == 0
    pl.semaphore_wait(barrier, jnp.where(leader, len(near) + GROUP, len(near)))
    previous = lax.rem(k + GROUPS - 1, GROUPS) * GROUP
    lead_copies = [
        pltpu.make_async_remote_copy(
            src_ref=halves.at[0, 1],
            dst_ref=following,
            send_sem=lead_send.at[i],
            recv_sem=lead_recv,
            device_id=(previous + i, j),
            device_id_type=MESH,
        )
        for i in range(GROUP)
    ]

    @pl.when(leader)
    def _():
        for copy in lead_copies:
            copy.start()

    group_copies = []
    for m in (7, 6, 3, 2, 5, 4, 1):
        copy = pltpu.make_async_remote_copy(
            src_ref=halves.at[g],
            dst_ref=halves.at[g],
            send_sem=group_send.at[m],
            recv_sem=group_recv.at[m],
            device_id=(member(m), j),
            device_id_type=MESH,
        )
        copy.start()
        group_copies.append(copy)
    for d in (-2, 2):
        pl.semaphore_signal(far_sem.at[0], inc=1, device_id=(column(d), j), device_id_type=MESH)

    ready = PORTIONS[0][1] // 2 * TILES
    lax.fori_loop(CHUNKS, ready, steer, 0)

    pl.semaphore_wait(far_sem.at[0], 2)
    for m in range(1, GROUP):
        pl.semaphore_signal(far_sem.at[1], inc=1, device_id=(member(m), j), device_id_type=MESH)

    for m in (1, 4, 5, 2, 3, 6, 7):
        slot = halves.at[flip(g, 3, m)]
        pltpu.make_async_remote_copy(
            src_ref=slot,
            dst_ref=slot,
            send_sem=group_send.at[m],
            recv_sem=group_recv.at[m],
            device_id=(member(m), j),
            device_id_type=MESH,
        ).wait_recv()
    lead_copies[0].wait_recv()

    for s in range(GROUP):
        if s < GROUP - 1:
            second = halves[s + 1, 1]
        else:
            second = jnp.where(k == GROUPS - 1, 0.0, following[...])
        wide[16 * s : 16 * s + 16, :] = halves[s, 0] + second
    for c in range(4):
        for b in range(NBINS):
            real = wide[pl.ds(4 * c + 2 * b, GROUP, stride=16), :]
            imag = wide[pl.ds(4 * c + 2 * b + 1, GROUP, stride=16), :]
            lanes = slice(128 * c, 128 * c + 128)
            sine_lanes = slice(LOCAL_MICS + 128 * c, LOCAL_MICS + 128 * c + 128)
            x_ref[b, :, lanes] = jnp.concatenate([real, imag], axis=0).astype(BF16)
            x_ref[b, :, sine_lanes] = jnp.concatenate([-imag, real], axis=0).astype(BF16)

    sum_copies = []
    for first, end in PORTIONS:
        if first:
            lax.fori_loop(first // 2 * TILES, end // 2 * TILES, steer, 0)
        lanes = slice(first * SHARE, end * SHARE)
        for b in range(NBINS):
            beam = jnp.dot(x_ref[b], w_ref[b, :, lanes], preferred_element_type=F32)
            for o in range(end - first):
                part[first + o, 16 * b : 16 * b + 16, :] = beam[:, o * SHARE : (o + 1) * SHARE]
        for o in range(first, min(end, OWNERS - 1)):
            copy = pltpu.make_async_remote_copy(
                src_ref=part.at[o],
                dst_ref=arrived.at[o],
                send_sem=sum_send.at[o],
                recv_sem=sum_recv.at[o],
                device_id=(t, owner(o)),
                device_id_type=MESH,
            )
            copy.start()
            sum_copies.append(copy)
    beam = part[OWNERS - 1]
    for o in range(OWNERS - 1):
        sum_copies[o].wait_recv()
        beam += arrived[o]
    squares = beam * beam
    folded = squares[0:8] + squares[8:16] + squares[16:24] + squares[24:32]
    final[t] = jnp.sum(folded, axis=0, keepdims=True)

    pl.semaphore_wait(far_sem.at[1], GROUP - 1)
    for d in sorted(range(1, SPANS), key=lambda d: -min(d, SPANS - d)):
        pltpu.make_async_remote_copy(
            src_ref=final.at[t],
            dst_ref=final.at[t],
            send_sem=final_send,
            recv_sem=final_recv,
            device_id=(lax.rem(t + d, SPANS), j),
            device_id_type=MESH,
        ).start()

    @pl.when(leader)
    def _():
        for copy in lead_copies:
            copy.wait_send()

    for copy in group_copies + sum_copies:
        copy.wait_send()
    others = final.at[pl.ds(0, SPANS - 1)]
    rest = pltpu.make_async_remote_copy(
        src_ref=others,
        dst_ref=others,
        send_sem=final_send,
        recv_sem=final_recv,
        device_id=(column(1), j),
        device_id_type=MESH,
    )
    rest.wait_send()
    rest.wait_recv()
    scale = 1.0 / (SPANS * NBINS * MICS)
    for i in range(GROUP):
        row = final[i]
        for n in range(1, GROUPS):
            row += final[GROUP * n + i]
        out_ref[i : i + 1, :] = row * scale


def local(signal, mic_pos, grid_pos, bins):
    dma = pltpu.SemaphoreType.DMA
    operands = [pltpu.with_memory_space_constraint(a, pltpu.HBM) for a in (signal, mic_pos, grid_pos, bins)]
    power = pl.pallas_call(
        kernel,
        out_shape=pltpu.VMEM((GROUP, SHARE), F32),
        in_specs=[pl.BlockSpec(memory_space=pl.ANY)] * 4,
        out_specs=pl.BlockSpec(memory_space=pltpu.VMEM),
        scratch_shapes=[
            pltpu.VMEM((SPAN, LOCAL_MICS), BF16),
            pltpu.VMEM(mic_pos.shape, jnp.int32),
            pltpu.VMEM(grid_pos.shape, jnp.int32),
            pltpu.SMEM(bins.shape, jnp.int32),
            pltpu.VMEM((LOCAL_MICS, 8), F32),
            pltpu.VMEM((8, POINTS), F32),
            pltpu.VMEM((GROUP, 2, 16, 128), F32),
            pltpu.VMEM((16, 128), F32),
            pltpu.VMEM((GROUP * 16, 128), F32),
            pltpu.VMEM((NBINS, 2 * GROUP, 2 * LOCAL_MICS), BF16),
            pltpu.VMEM((NBINS, 2 * LOCAL_MICS, POINTS), BF16),
            pltpu.VMEM((OWNERS, 4 * GROUP, SHARE), F32),
            pltpu.VMEM((OWNERS, 4 * GROUP, SHARE), F32),
            pltpu.VMEM((SPANS, 1, SHARE), F32),
            dma((CHUNKS,)),
            dma((3,)),
            dma((GROUP,)),
            dma,
            dma((GROUP,)),
            dma((GROUP,)),
            dma((OWNERS,)),
            dma((OWNERS,)),
            dma,
            dma,
            pltpu.SemaphoreType.REGULAR((2,)),
        ],
        compiler_params=pltpu.CompilerParams(
            collective_id=0, has_side_effects=True, vmem_limit_bytes=32 * 1024 * 1024
        ),
    )(*operands)
    return power.reshape(-1)


def solution(mesh):
    in_specs = (P("tm", "mic"), P(None, "mic"), P(), P())
    out_specs = P("mic")
    return jax.shard_map(local, mesh=mesh, in_specs=in_specs, out_specs=out_specs, check_vma=False)
```

```python
import math

import jax
import jax.numpy as jnp
from jax import lax
from jax.experimental import pallas as pl
from jax.experimental.pallas import tpu as pltpu
from jax.sharding import PartitionSpec as P

MESH = pl.DeviceIdType.MESH
F32 = jnp.float32
BF16 = jnp.bfloat16

MICS = 4096
SEGLEN = 8192
NBINS = 2
SPAN = 4096
LOCAL_MICS = 512
SPANS = 64
GROUP = 8
GROUPS = SPANS // GROUP
OWNERS = 8
SHARE = 128
POINTS = OWNERS * SHARE
CHUNKS = 8
CHUNK = SPAN // CHUNKS
TILE = 64
PAIR = 2 * SHARE
TILES = LOCAL_MICS // TILE
STEPS = TILES * OWNERS // 2
PORTIONS = ((0, 2), (2, 6), (6, 8))

UNIT = 544.5
SINE = (-0.020778089505148072, 0.22160904131003262, -0.7069151550432146, 1.0)
COSINE = (0.0025972698674584724, -0.08311238928243203, 0.4432205811375266, -0.9426014873154713, 1.0)
SINE_FINE = (
    0.707106764602781,
    -0.029462748844770903,
    0.0003682655953189757,
    -2.1877062853298923e-06,
    7.155046293945055e-09,
)
TURN = 2.0 * math.pi
TURN_HIGH = 6.28125
TURN_LOW = TURN - TURN_HIGH
ROUNDER = 1.5 * 2.0**23


def poly(coefficients, x):
    value = x if coefficients[-1] == 1.0 else coefficients[-1] * x
    value = value + coefficients[-2]
    for c in coefficients[-3::-1]:
        value = value * x + c
    return value


def half_sine(f):
    return f * poly(SINE_FINE, f * f)


def table_chunk(index, bin_a, bin_b):
    row = lax.broadcasted_iota(jnp.int32, (8, CHUNK), 0)
    lane = lax.broadcasted_iota(jnp.int32, (8, CHUNK), 1)
    k = jnp.where((row & 2) == 0, bin_a, bin_b)
    sample = lane + index * CHUNK + (row >> 2) * SPAN
    phase = (k * sample + (row & 1) * (SEGLEN // 4)) & (SEGLEN - 1)
    s = half_sine((phase - SEGLEN // 2).astype(F32) * (TURN / SEGLEN))
    near = jnp.minimum(sample, SEGLEN - sample).astype(F32)
    w = half_sine(near * (TURN / SEGLEN))
    weighting = (0.5 / math.sqrt(0.375 * SEGLEN)) * (w * w)
    return (weighting * (s * s - 1.0)).astype(BF16)


def flip(index, bits, mask):
    value = 0
    for bit in range(bits):
        digit = (index // (1 << bit)) % 2
        value = value + (1 << bit) * (1 - digit if mask >> bit & 1 else digit)
    return value


def kernel(
    sig_hbm,
    mic_hbm,
    grid_hbm,
    bins_hbm,
    out_ref,
    sig,
    mic,
    grid,
    bins,
    mic_columns,
    grid_rows,
    halves,
    following,
    wide,
    x_ref,
    w_ref,
    part,
    arrived,
    final,
    sig_sem,
    small_sem,
    lead_send,
    lead_recv,
    group_send,
    group_recv,
    sum_send,
    sum_recv,
    final_send,
    final_recv,
    far_sem,
):
    t, j = lax.axis_index("tm"), lax.axis_index("mic")
    k, g = t // GROUP, t % GROUP

    def member(mask):
        return k * GROUP + flip(g, 3, mask)

    def owner(place):
        across, along = ((1, 2), (1, 1), (1, 3), (0, 2), (1, 0), (0, 1), (0, 3), (0, 0))[place]
        return flip(j // 4, 1, across) * 4 + lax.rem(j + along, 4)

    def column(d):
        return lax.rem(t + SPANS + d * GROUP, SPANS)

    small = [
        pltpu.make_async_copy(bins_hbm, bins, small_sem.at[0]),
        pltpu.make_async_copy(mic_hbm, mic, small_sem.at[1]),
        pltpu.make_async_copy(grid_hbm, grid, small_sem.at[2]),
    ]
    for copy in small:
        copy.start()
    loads = []
    for c in range(CHUNKS):
        rows = pl.ds(c * CHUNK, CHUNK)
        loads.append(pltpu.make_async_copy(sig_hbm.at[rows], sig.at[rows], sig_sem.at[c]))
        loads[-1].start()

    barrier = pltpu.get_barrier_semaphore()
    next_leader = lax.rem(k + 1, GROUPS) * GROUP
    near = [(column(d), j) for d in (-2, 2, -1, 1)]
    near += [(member(m), j) for m in (7, 6, 3, 2, 5, 4, 1)]
    near += [(t, lax.rem(j + d, OWNERS)) for d in range(1, OWNERS)]
    for peer in [(next_leader, j)] + near:
        pl.semaphore_signal(barrier, inc=1, device_id=peer, device_id_type=MESH)

    small[0].wait()
    bin_a, bin_b = bins[0], bins[1]
    tables = [table_chunk(c, bin_a, bin_b) for c in range(CHUNKS)]

    small[1].wait()
    small[2].wait()
    padded = jnp.concatenate([mic[...].astype(F32), jnp.zeros((5, LOCAL_MICS), F32)], axis=0)
    mic_columns[...] = padded.T
    for o in range(OWNERS):
        start = pl.multiple_of((owner(o) * GROUP + g) * SHARE, SHARE)
        for coordinate in range(3):
            row = grid[coordinate : coordinate + 1, pl.ds(start, SHARE)].astype(F32)
            grid_rows[coordinate : coordinate + 1, o * SHARE : (o + 1) * SHARE] = row

    bin_values = (bin_a.astype(F32), bin_b.astype(F32))

    def steer(step, carry):
        tile, pair = step % TILES, step // TILES
        rows = pl.ds(pl.multiple_of(tile * TILE, TILE), TILE)
        sine_rows = pl.ds(pl.multiple_of(tile * TILE + LOCAL_MICS, TILE), TILE)
        lanes = pl.ds(pl.multiple_of(pair * PAIR, PAIR), PAIR)
        square = None
        for coordinate in range(3):
            column = mic_columns[rows, coordinate : coordinate + 1]
            offset = grid_rows[coordinate : coordinate + 1, lanes] - column
            square = offset * offset if square is None else square + offset * offset
        inverse = lax.rsqrt(square)
        distance = square * inverse
        strength = 16.0 * inverse
        weight = (16.0 * UNIT * UNIT) * inverse
        for b in range(NBINS):
            angle = (bin_values[b] * distance) * (-TURN / 8192.0)
            turns = (angle * (16.0 / TURN) + ROUNDER) - ROUNDER
            h = (angle - turns * (TURN_HIGH / 16.0)) - turns * (TURN_LOW / 16.0)
            h2 = h * h
            s = h * poly(SINE, h2)
            c = poly(COSINE, h2)
            scaled = weight * s
            w_ref[b, rows, lanes] = (strength - scaled * s).astype(BF16)
            w_ref[b, sine_rows, lanes] = (scaled * c).astype(BF16)
        return carry

    total = jnp.zeros((8, LOCAL_MICS), F32)
    for c in range(CHUNKS):
        loads[c].wait()
        total += jnp.dot(tables[c], sig[c * CHUNK : (c + 1) * CHUNK, :], preferred_element_type=F32)
        steer(c, 0)
    for c in range(4):
        block = total[:, c * 128 : (c + 1) * 128]
        halves[g, 0, 4 * c : 4 * c + 4, :] = block[0:4]
        halves[g, 1, 4 * c : 4 * c + 4, :] = block[4:8]

    leader = g == 0
    pl.semaphore_wait(barrier, jnp.where(leader, len(near) + GROUP, len(near)))
    previous = lax.rem(k + GROUPS - 1, GROUPS) * GROUP
    lead_copies = [
        pltpu.make_async_remote_copy(
            src_ref=halves.at[0, 1],
            dst_ref=following,
            send_sem=lead_send.at[i],
            recv_sem=lead_recv,
            device_id=(previous + i, j),
            device_id_type=MESH,
        )
        for i in range(GROUP)
    ]

    @pl.when(leader)
    def _():
        for copy in lead_copies:
            copy.start()

    for m in (7, 6, 3, 2, 5, 4, 1):
        copy = pltpu.make_async_remote_copy(
            src_ref=halves.at[g],
            dst_ref=halves.at[g],
            send_sem=group_send,
            recv_sem=group_recv,
            device_id=(member(m), j),
            device_id_type=MESH,
        )
        copy.start()
    for d in (-2, 2):
        pl.semaphore_signal(far_sem.at[0], inc=1, device_id=(column(d), j), device_id_type=MESH)

    ready = PORTIONS[-1][0] // 2 * TILES
    lax.fori_loop(CHUNKS, ready, steer, 0, unroll=2)

    pl.semaphore_wait(far_sem.at[0], 2)
    for m in range(1, GROUP):
        pl.semaphore_signal(far_sem.at[1], inc=1, device_id=(member(m), j), device_id_type=MESH)

    slots = halves.at[pl.ds(0, GROUP - 1)]
    members = pltpu.make_async_remote_copy(
        src_ref=slots,
        dst_ref=slots,
        send_sem=group_send,
        recv_sem=group_recv,
        device_id=(member(1), j),
        device_id_type=MESH,
    )
    members.wait_recv()
    lead_copies[0].wait_recv()

    for s in range(GROUP):
        if s < GROUP - 1:
            second = halves[s + 1, 1]
        else:
            second = jnp.where(k == GROUPS - 1, 0.0, following[...])
        wide[16 * s : 16 * s + 16, :] = halves[s, 0] + second
    for c in range(4):
        for b in range(NBINS):
            real = wide[pl.ds(4 * c + 2 * b, GROUP, stride=16), :]
            imag = wide[pl.ds(4 * c + 2 * b + 1, GROUP, stride=16), :]
            lanes = slice(128 * c, 128 * c + 128)
            sine_lanes = slice(LOCAL_MICS + 128 * c, LOCAL_MICS + 128 * c + 128)
            x_ref[b, :, lanes] = jnp.concatenate([real, imag], axis=0).astype(BF16)
            x_ref[b, :, sine_lanes] = jnp.concatenate([-imag, real], axis=0).astype(BF16)

    sum_copies = []
    for first, end in PORTIONS:
        if end == OWNERS:
            lax.fori_loop(first // 2 * TILES, end // 2 * TILES, steer, 0, unroll=2)
        lanes = slice(first * SHARE, end * SHARE)
        for b in range(NBINS):
            beam = jnp.dot(x_ref[b], w_ref[b, :, lanes], preferred_element_type=F32)
            for o in range(end - first):
                part[first + o, 16 * b : 16 * b + 16, :] = beam[:, o * SHARE : (o + 1) * SHARE]
        for o in range(first, min(end, OWNERS - 1)):
            copy = pltpu.make_async_remote_copy(
                src_ref=part.at[o],
                dst_ref=arrived.at[o],
                send_sem=sum_send.at[o],
                recv_sem=sum_recv.at[o],
                device_id=(t, owner(o)),
                device_id_type=MESH,
            )
            copy.start()
            sum_copies.append(copy)
    beam = part[OWNERS - 1]
    for o in range(OWNERS - 1):
        sum_copies[o].wait_recv()
        beam += arrived[o]
    squares = beam * beam
    folded = squares[0:8] + squares[8:16] + squares[16:24] + squares[24:32]
    final[t] = jnp.sum(folded, axis=0, keepdims=True)

    pl.semaphore_wait(far_sem.at[1], GROUP - 1)
    for d in sorted(range(1, SPANS), key=lambda d: -min(d, SPANS - d)):
        pltpu.make_async_remote_copy(
            src_ref=final.at[t],
            dst_ref=final.at[t],
            send_sem=final_send,
            recv_sem=final_recv,
            device_id=(lax.rem(t + d, SPANS), j),
            device_id_type=MESH,
        ).start()

    @pl.when(leader)
    def _():
        for copy in lead_copies:
            copy.wait_send()

    members.wait_send()
    for copy in sum_copies:
        copy.wait_send()
    others = final.at[pl.ds(0, SPANS - 1)]
    rest = pltpu.make_async_remote_copy(
        src_ref=others,
        dst_ref=others,
        send_sem=final_send,
        recv_sem=final_recv,
        device_id=(column(1), j),
        device_id_type=MESH,
    )
    rest.wait_send()
    rest.wait_recv()
    scale = 1.0 / (SPANS * NBINS * MICS)
    for i in range(GROUP):
        row = final[i]
        for n in range(1, GROUPS):
            row += final[GROUP * n + i]
        out_ref[i : i + 1, :] = row * scale


def local(signal, mic_pos, grid_pos, bins):
    dma = pltpu.SemaphoreType.DMA
    operands = [pltpu.with_memory_space_constraint(a, pltpu.HBM) for a in (signal, mic_pos, grid_pos, bins)]
    power = pl.pallas_call(
        kernel,
        out_shape=pltpu.VMEM((GROUP, SHARE), F32),
        in_specs=[pl.BlockSpec(memory_space=pl.ANY)] * 4,
        out_specs=pl.BlockSpec(memory_space=pltpu.VMEM),
        scratch_shapes=[
            pltpu.VMEM((SPAN, LOCAL_MICS), BF16),
            pltpu.VMEM(mic_pos.shape, jnp.int32),
            pltpu.VMEM(grid_pos.shape, jnp.int32),
            pltpu.SMEM(bins.shape, jnp.int32),
            pltpu.VMEM((LOCAL_MICS, 8), F32),
            pltpu.VMEM((8, POINTS), F32),
            pltpu.VMEM((GROUP, 2, 16, 128), F32),
            pltpu.VMEM((16, 128), F32),
            pltpu.VMEM((GROUP * 16, 128), F32),
            pltpu.VMEM((NBINS, 2 * GROUP, 2 * LOCAL_MICS), BF16),
            pltpu.VMEM((NBINS, 2 * LOCAL_MICS, POINTS), BF16),
            pltpu.VMEM((OWNERS, 4 * GROUP, SHARE), F32),
            pltpu.VMEM((OWNERS, 4 * GROUP, SHARE), F32),
            pltpu.VMEM((SPANS, 1, SHARE), F32),
            dma((CHUNKS,)),
            dma((3,)),
            dma((GROUP,)),
            dma,
            dma,
            dma,
            dma((OWNERS,)),
            dma((OWNERS,)),
            dma,
            dma,
            pltpu.SemaphoreType.REGULAR((2,)),
        ],
        compiler_params=pltpu.CompilerParams(
            collective_id=0, has_side_effects=True, vmem_limit_bytes=32 * 1024 * 1024
        ),
    )(*operands)
    return power.reshape(-1)


def solution(mesh):
    in_specs = (P("tm", "mic"), P(None, "mic"), P(), P())
    out_specs = P("mic")
    return jax.shard_map(local, mesh=mesh, in_specs=in_specs, out_specs=out_specs, check_vma=False)
```
